256 devices in a mesh: dp: 16 (over y, x), fsdp: 16 (over z, core).
Axes of the slice: x: 4, y: 4, z: 8, core: 2. Of those that a mesh axis runs over, the one named last changes fastest.
Arguments:
- hidden: bfloat16 [16, 16, 2, 128, 14336], P('dp', 'fsdp'), may hold values from -6 to 6
- cotangent: bfloat16 [16, 16, 2, 128, 1792], P('dp', 'fsdp'), may hold values from -20 to 20
- counts: int32 [16, 16], P('dp', 'fsdp'), may hold values from 0 to 2, as said below
- noise: float32 [14336, 1792], P(('dp', 'fsdp')), may hold values from -224 to 224
Outputs:
- gradient: float32 [14336, 1792], P(('dp', 'fsdp'))
The draws below stay inside these ranges and needn't reach their ends.
Inputs may be any that keep to these rules, and one draw needn't show every extreme that they name: On every fsdp index, the counts of the first j dp indices sum to j * 1 plus 0 to 1, and the counts of all dp indices sum to exactly 1 times the number of dp indices. A device's examples fill its slots from slot 0.
All inputs are finite; a program needn't handle non-finite values.
Results may differ from the reference program's by a relative error of at most 0.0025.
Values may be sent and summed in bfloat16 or wider, within the bound.
No kernel may reach another device: no remote copies, remote signals or barrier semaphores. Data moves between devices by JAX's collectives and lax.ppermute only.
A program may use at most 128 MiB of HBM per device.

```python
import math
import jax
import jax.numpy as jnp
from jax import lax

D = 1792
F = 14336
L = 128
BAL = 1
POOL = 2
EXPECTED_BATCH = 256
N_DP = 16
N_FSDP = 16


def draw_cotangent(key, part):
    key = jax.random.fold_in(key, 11)
    scale_key, value_key = jax.random.split(key, 2)
    example_scale = jnp.exp(jax.random.uniform(scale_key, (N_DP, N_FSDP, POOL, 1, 1), jnp.float32, math.log(0.25), math.log(4.0)))
    values = jax.random.truncated_normal(value_key, -5.0, 5.0, (N_DP, N_FSDP, POOL, L, D), jnp.float32)
    return (example_scale * values).astype(jnp.bfloat16)


def draw_counts(key, part):
    key = jax.random.fold_in(key, 23)
    move_key, peak_key = jax.random.split(key)
    movers = jax.random.randint(move_key, (N_DP, N_FSDP), 0, BAL + 1)
    position = jnp.arange(N_DP, dtype=jnp.int32)[:, None]
    peak_row = jax.random.randint(peak_key, (1, N_FSDP), 0, N_DP - 1)
    movers = jnp.where(position == peak_row, BAL, movers)
    movers = jnp.where(position == peak_row - 1, 0, movers)
    movers = jnp.where(position == N_DP - 1, 0, movers)
    previous = jnp.concatenate([jnp.zeros((1, N_FSDP), jnp.int32), movers[:-1]], 0)
    return (BAL + movers - previous).astype(jnp.int32)


def steps_of(stream_key, dims, cuts, least, high):
    level = 1.0
    for dim, blocks in cuts:
        heights = jax.random.uniform(jax.random.fold_in(jax.random.fold_in(stream_key, 6), dim), (blocks,), jnp.float32, least / len(cuts), high / len(cuts))
        level = level * jnp.repeat(jnp.exp(heights), dims[dim] // blocks).reshape((-1,) + (1,) * (len(dims) - 1 - dim))
    return level


def centred(key, dims, deviation, most, pieces=(), kind=jnp.bfloat16):
    array = deviation * jax.random.normal(key, dims, jnp.float32)
    if pieces:
        array = array * steps_of(key, dims, pieces, -0.22, 0.18)
    return jnp.clip(array, -most, most).astype(kind)


def setup_inputs(seed: int = 0) -> dict:
    key_of = jax.random.split(jax.random.key(seed), 5)
    return {
        "hidden": centred(key_of[0], (N_DP, N_FSDP, POOL, L, F), 1.0, 6.0, ((0, 16), (1, 16))),
        "cotangent": draw_cotangent(jax.random.fold_in(key_of[4], 71), 0),
        "counts": draw_counts(jax.random.fold_in(key_of[4], 71), 0),
        "noise": centred(key_of[3], (F, D), (0.2 * (L * EXPECTED_BATCH) ** 0.5), 224.0, ((0, 256),), jnp.float32),
    }


def clip_factors(hidden_rows, cotangent_matrix_rows, live_slots):
    clipping_threshold = math.sqrt(L * F * D)
    hidden_wide = hidden_rows.astype(jnp.float32)
    cotangent_full_width = cotangent_matrix_rows.astype(jnp.float32)
    hidden_gram_matrix = jnp.einsum('slf,smf->slm', hidden_wide, hidden_wide)
    cotangent_gram_matrix = jnp.einsum('ogj,oij->ogi', cotangent_full_width, cotangent_full_width)
    norm_values = jnp.sqrt(lax.optimization_barrier(jnp.sum(hidden_gram_matrix * cotangent_gram_matrix, axis=(1, 2))))
    return jnp.where(live_slots, clipping_threshold / jnp.maximum(norm_values, clipping_threshold), jnp.float32(0.0))

def reference(hidden, cotangent, counts, noise):
    slot_index = jnp.arange(POOL, dtype=jnp.int32)
    live_slots = slot_index[None, None, :] < counts[:, :, None]

    def add_row(gradient_total, row_items):
        row_hidden, row_cotangent, row_live = row_items
        flat_hidden = row_hidden.reshape(-1, L, F)
        flat_cotangent = row_cotangent.reshape(-1, L, D)
        factors = clip_factors(flat_hidden, flat_cotangent, row_live.reshape(-1))
        weighted = (factors[:, None, None] * flat_cotangent.astype(jnp.float32)).astype(jnp.bfloat16)
        row_term = jnp.dot(flat_hidden.reshape(-1, F).T, weighted.reshape(-1, D), preferred_element_type=jnp.float32)
        return (gradient_total + row_term, None)
    gradient_total, unused = lax.scan(add_row, jnp.zeros((F, D), jnp.float32), (hidden, cotangent, live_slots))
    return (gradient_total + noise) / (N_DP * N_FSDP * BAL)
```

```python
import math

import jax
import jax.numpy as jnp
from jax import lax
from jax.experimental import pallas as pl
from jax.experimental.pallas import tpu as pltpu
from jax.sharding import PartitionSpec as P

D = 1792
F = 14336
L = 128
BAL = 1
POOL = 2
N_DP = 16
N_FSDP = 16
CORES = 2
NZ = N_FSDP // CORES
TOK = POOL * L
BLOCK = F // N_DP
ROWS = BLOCK // N_FSDP
LIVE = N_DP * BAL
TILE = 256
QUARTERS = 4
WIDTHS = (1024, 768)
CLIP = math.sqrt(L * F * D)
VMEM = 58 * 2**20


def prepare_kernel(count_ref, hidden_ref, cotangent_ref, blocks_ref, factor_ref, rows_buf, other_buf, gram, sems):
    def load(d):
        return pltpu.make_async_copy(
            hidden_ref.at[:, :, pl.ds(pl.multiple_of(d * BLOCK, L), BLOCK)], rows_buf.at[d], sems.at[0, d]
        )

    def store(d):
        return pltpu.make_async_copy(rows_buf.at[d], blocks_ref.at[d], sems.at[1, d])

    second = pltpu.make_async_copy(cotangent_ref, other_buf, sems.at[2, 0])
    for d in range(N_DP):
        load(d).start()
    second.start()
    gram[...] = jnp.zeros_like(gram)

    def step(d, carry):
        load(d).wait()
        store(d).start()
        rows = rows_buf[d].reshape(TOK, BLOCK)
        gram[...] += lax.dot_general(
            rows, rows, (((1,), (1,)), ((), ())), preferred_element_type=jnp.float32
        )
        return carry

    lax.fori_loop(0, N_DP, step, 0)
    second.wait()
    held = count_ref[0, 0]
    rows = other_buf[...].reshape(TOK, D)
    other = lax.dot_general(rows, rows, (((1,), (1,)), ((), ())), preferred_element_type=jnp.float32)
    both = gram[...] * other
    lane = lax.broadcasted_iota(jnp.int32, (8, L), 1)
    factors = jnp.zeros((8, L), jnp.float32)
    for s in range(POOL):
        span = slice(s * L, (s + 1) * L)
        squared = jnp.sum(both[span, span], axis=(0, 1), keepdims=True)
        norm = jnp.sqrt(jnp.maximum(squared, 0.0))
        factor = CLIP / jnp.maximum(norm, CLIP)
        factor = jnp.where(s < held, factor, jnp.zeros_like(factor))
        factors = jnp.where(lane == s, factor, factors)
    for d in range(N_DP):
        factor_ref[d] = factors
    for d in range(N_DP):
        store(d).wait()


def prepare(hidden, cotangent, held):
    anywhere = pl.BlockSpec(memory_space=pl.ANY)
    whole = pl.BlockSpec(memory_space=pltpu.VMEM)
    return pl.pallas_call(
        prepare_kernel,
        in_specs=[pl.BlockSpec(memory_space=pltpu.SMEM), anywhere, anywhere],
        out_specs=[anywhere, whole],
        out_shape=[
            jax.ShapeDtypeStruct((N_DP, POOL, L, BLOCK), jnp.bfloat16),
            jax.ShapeDtypeStruct((N_DP, 8, L), jnp.float32),
        ],
        scratch_shapes=[
            pltpu.VMEM((N_DP, POOL, L, BLOCK), jnp.bfloat16),
            pltpu.VMEM((POOL, L, D), jnp.bfloat16),
            pltpu.VMEM((TOK, TOK), jnp.float32),
            pltpu.SemaphoreType.DMA((3, N_DP)),
        ],
        compiler_params=pltpu.CompilerParams(vmem_limit_bytes=VMEM),
        cost_estimate=pl.CostEstimate(
            flops=2 * TOK * L * F, bytes_accessed=4 * TOK * F, transcendentals=0
        ),
        name="prepare",
    )(held, hidden, cotangent)


def turn_kernel(place_ref, blocks_ref, out_ref):
    out_ref[...] = blocks_ref[0].T


def turn(place, blocks):
    return pl.pallas_call(
        turn_kernel,
        grid_spec=pltpu.PrefetchScalarGridSpec(
            num_scalar_prefetch=1,
            grid=(LIVE,),
            in_specs=[
                pl.BlockSpec(
                    (1, L, BLOCK), lambda e, place_ref: (place_ref[e] // POOL, place_ref[e] % POOL, 0)
                )
            ],
            out_specs=pl.BlockSpec((BLOCK, L), lambda e, place_ref: (0, e)),
        ),
        out_shape=jax.ShapeDtypeStruct((BLOCK, LIVE * L), jnp.bfloat16),
        compiler_params=pltpu.CompilerParams(vmem_limit_bytes=VMEM),
        cost_estimate=pl.CostEstimate(flops=0, bytes_accessed=4 * LIVE * L * BLOCK, transcendentals=0),
        name="turn",
    )(place, blocks)


def product_kernel(core_ref, factor_ref, turned_ref, *refs):
    quarters, out_refs, (weighted, total) = refs[:QUARTERS], refs[QUARTERS:-2], refs[-2:]
    for q, ref in enumerate(quarters):
        for k in range(LIVE // QUARTERS):
            e = q * (LIVE // QUARTERS) + k
            rows = ref[k * L : (k + 1) * L, :].astype(jnp.float32)
            weighted[e * L : (e + 1) * L, :] = (factor_ref[e] * rows).astype(jnp.bfloat16)
    total[...] = jnp.dot(turned_ref[...], weighted[...], preferred_element_type=jnp.float32)
    core = core_ref[0]
    start = 0
    for c, width in enumerate(WIDTHS):
        end = start + width // TILE

        @pl.when((pl.program_id(0) >= start) & (pl.program_id(0) < end))
        def _(keep_ref=out_refs[2 * c], send_ref=out_refs[2 * c + 1]):
            for z in range(NZ):
                base = z * CORES * ROWS
                mine = pl.multiple_of(base + core * ROWS, 8)
                others = pl.multiple_of(base + (1 - core) * ROWS, 8)
                keep_ref[z] = total[pl.ds(mine, ROWS), :]
                send_ref[z] = total[pl.ds(others, ROWS), :]

        start = end


def product(core, factors, turned, cotangents):
    scalars = pl.BlockSpec(memory_space=pltpu.SMEM)
    out_specs, out_shape = [], []
    start = 0
    for width in WIDTHS:
        tiles = width // TILE

        def at(i, start=start, tiles=tiles):
            return (0, 0, jnp.clip(i - start, 0, tiles - 1))

        out_specs += [pl.BlockSpec((NZ, ROWS, TILE), at)] * 2
        out_shape += [jax.ShapeDtypeStruct((NZ, ROWS, width), jnp.float32)] * 2
        start += tiles
    return pl.pallas_call(
        product_kernel,
        grid=(D // TILE,),
        in_specs=[scalars, scalars, pl.BlockSpec((BLOCK, LIVE * L), lambda i: (0, 0))]
        + [
            pl.BlockSpec((LIVE * L // QUARTERS, TILE), lambda i, q=q: (q, i)) for q in range(QUARTERS)
        ],
        out_specs=out_specs,
        out_shape=out_shape,
        scratch_shapes=[
            pltpu.VMEM((LIVE * L, TILE), jnp.bfloat16),
            pltpu.VMEM((BLOCK, TILE), jnp.float32),
        ],
        compiler_params=pltpu.CompilerParams(vmem_limit_bytes=VMEM),
        cost_estimate=pl.CostEstimate(
            flops=2 * LIVE * L * BLOCK * D, bytes_accessed=24 * 2**20, transcendentals=0
        ),
        name="product",
    )(core, factors, turned, *[cotangents] * QUARTERS)


def around_z(step):
    return [(i, (i + step * CORES) % N_FSDP) for i in range(N_FSDP)]


def other_core(send):
    return lax.ppermute(send, "fsdp", [(i, i ^ 1) for i in range(N_FSDP)])


def reduce_begin(keep, got):
    z = lax.axis_index("fsdp") // CORES

    def own(offset):
        at = (z + offset) % NZ
        return lax.dynamic_index_in_dim(keep, at, 0, False) + lax.dynamic_index_in_dim(got, at, 0, False)

    half = keep.shape[2] // 2
    far = own(NZ // 2)
    up = lax.ppermute(far[:, :half], "fsdp", around_z(1))
    down = lax.ppermute(far[:, half:], "fsdp", around_z(-1))
    up = jnp.concatenate([up, jnp.zeros_like(up)], 1) + own(NZ // 2 - 1)
    down = jnp.concatenate([jnp.zeros_like(down), down], 1) + own(1 - NZ // 2)
    return own, up, down


def reduce_step(own, up, down, offset):
    up = lax.ppermute(up, "fsdp", around_z(1))
    down = lax.ppermute(down, "fsdp", around_z(-1))
    if offset:
        return up + own(offset), down + own(-offset)
    return up + down + own(0)


def across_dp(value):
    return lax.all_to_all(value, "dp", split_axis=0, concat_axis=0, tiled=True)


def body(hidden, cotangent, counts, noise):
    me = lax.axis_index("dp")
    hidden, cotangent = hidden[0, 0], cotangent[0, 0]
    last = lax.dynamic_index_in_dim(cotangent, jnp.clip(counts[0, 0] - 1, 0, POOL - 1), 0, False)
    last, hidden, counts = lax.optimization_barrier((last, hidden, counts))
    passed = lax.ppermute(last, "dp", [(i, (i + 1) % N_DP) for i in range(N_DP)])
    held = across_dp(jnp.broadcast_to(counts[:, :, None], (N_DP, 8, L)))[:, 0, 0]
    blocks, factors = prepare(hidden, cotangent, counts)

    index = jnp.arange(N_DP, dtype=jnp.int32)
    before = jnp.sum(jnp.where(index[None, :] < index[:, None], held[None, :], 0), axis=1)
    left = jnp.sum(jnp.where(index[None, :] == index[:, None] - 1, held[None, :], 0), axis=1)
    shifted = before > index * BAL
    place = jnp.where(
        shifted,
        jnp.maximum(index - 1, 0) * POOL + jnp.clip(left - 1, 0, POOL - 1),
        index * POOL,
    )
    mine_shifted = jnp.sum(jnp.where(index == me, shifted.astype(jnp.int32), 0)) > 0
    chosen = jnp.where(mine_shifted, passed, cotangent[0])

    chosen, blocks, place, factors = lax.optimization_barrier((chosen, blocks, place, factors))
    cotangents = lax.all_gather(chosen, "dp", axis=0, tiled=True)
    blocks = across_dp(blocks.reshape(N_DP, TOK, BLOCK))
    blocks, factors, place = lax.optimization_barrier((blocks, factors, place))
    factors = across_dp(factors)[:, 0, :POOL].reshape(-1)
    factors = jnp.sum(
        jnp.where(place[:, None] == jnp.arange(N_DP * POOL)[None, :], factors[None, :], 0.0), axis=1
    )
    turned = turn(place, blocks)
    core = (lax.axis_index("fsdp") % CORES).astype(jnp.int32).reshape(1)
    core, factors, turned, cotangents = lax.optimization_barrier((core, factors, turned, cotangents))
    chunks = product(core, factors, turned, cotangents)
    parts = [reduce_begin(keep, other_core(send)) for keep, send in zip(chunks[::2], chunks[1::2])]
    for offset in (2, 1, 0):
        sums = []
        for own, up, down in parts:
            sums.append(reduce_step(own, up, down, offset))
        parts = [(own, *moved) for (own, _, _), moved in zip(parts, sums)] if offset else sums
    return (jnp.concatenate(parts, 1) + noise) / (N_DP * N_FSDP * BAL)


def solution(mesh):
    in_specs = (
        P("dp", "fsdp", None, None, None),
        P("dp", "fsdp", None, None, None),
        P("dp", "fsdp"),
        P(("dp", "fsdp"), None),
    )
    out_specs = P(("dp", "fsdp"), None)
    return jax.shard_map(body, mesh=mesh, in_specs=in_specs, out_specs=out_specs, check_vma=False)
```

```python
import math

import jax
import jax.numpy as jnp
from jax import lax
from jax.experimental import pallas as pl
from jax.experimental.pallas import tpu as pltpu
from jax.sharding import PartitionSpec as P

D = 1792
F = 14336
L = 128
BAL = 1
POOL = 2
N_DP = 16
N_FSDP = 16
CORES = 2
NZ = N_FSDP // CORES
TOK = POOL * L
BLOCK = F // N_DP
ROWS = BLOCK // N_FSDP
LIVE = N_DP * BAL
TILE = 256
QUARTERS = 4
WIDTHS = (768, 1024)
CLIP = math.sqrt(L * F * D)
VMEM = 58 * 2**20


def prepare_kernel(count_ref, hidden_ref, cotangent_ref, blocks_ref, factor_ref, rows_buf, other_buf, gram, sems):
    def load(d):
        return pltpu.make_async_copy(
            hidden_ref.at[:, :, pl.ds(pl.multiple_of(d * BLOCK, L), BLOCK)], rows_buf.at[d], sems.at[0, d]
        )

    def store(d):
        return pltpu.make_async_copy(rows_buf.at[d], blocks_ref.at[d], sems.at[1, d])

    second = pltpu.make_async_copy(cotangent_ref, other_buf, sems.at[2, 0])
    for d in range(N_DP):
        load(d).start()
    second.start()
    gram[...] = jnp.zeros_like(gram)

    def step(d, carry):
        load(d).wait()
        store(d).start()
        rows = rows_buf[d].reshape(TOK, BLOCK)
        gram[...] += lax.dot_general(
            rows, rows, (((1,), (1,)), ((), ())), preferred_element_type=jnp.float32
        )
        return carry

    lax.fori_loop(0, N_DP, step, 0)
    second.wait()
    held = count_ref[0, 0]
    rows = other_buf[...].reshape(TOK, D)
    other = lax.dot_general(rows, rows, (((1,), (1,)), ((), ())), preferred_element_type=jnp.float32)
    both = gram[...] * other
    lane = lax.broadcasted_iota(jnp.int32, (8, L), 1)
    factors = jnp.zeros((8, L), jnp.float32)
    for s in range(POOL):
        span = slice(s * L, (s + 1) * L)
        squared = jnp.sum(both[span, span], axis=(0, 1), keepdims=True)
        norm = jnp.sqrt(jnp.maximum(squared, 0.0))
        factor = CLIP / jnp.maximum(norm, CLIP)
        factor = jnp.where(s < held, factor, jnp.zeros_like(factor))
        factors = jnp.where(lane == s, factor, factors)
    for d in range(N_DP):
        factor_ref[d] = factors
    for d in range(N_DP):
        store(d).wait()


def prepare(hidden, cotangent, held):
    anywhere = pl.BlockSpec(memory_space=pl.ANY)
    whole = pl.BlockSpec(memory_space=pltpu.VMEM)
    return pl.pallas_call(
        prepare_kernel,
        in_specs=[pl.BlockSpec(memory_space=pltpu.SMEM), anywhere, anywhere],
        out_specs=[anywhere, whole],
        out_shape=[
            jax.ShapeDtypeStruct((N_DP, POOL, L, BLOCK), jnp.bfloat16),
            jax.ShapeDtypeStruct((N_DP, 8, L), jnp.float32),
        ],
        scratch_shapes=[
            pltpu.VMEM((N_DP, POOL, L, BLOCK), jnp.bfloat16),
            pltpu.VMEM((POOL, L, D), jnp.bfloat16),
            pltpu.VMEM((TOK, TOK), jnp.float32),
            pltpu.SemaphoreType.DMA((3, N_DP)),
        ],
        compiler_params=pltpu.CompilerParams(vmem_limit_bytes=VMEM),
        cost_estimate=pl.CostEstimate(
            flops=2 * TOK * L * F, bytes_accessed=4 * TOK * F, transcendentals=0
        ),
        name="prepare",
    )(held, hidden, cotangent)


def turn_kernel(place_ref, blocks_ref, out_ref):
    out_ref[...] = blocks_ref[0].T


def turn(place, blocks):
    return pl.pallas_call(
        turn_kernel,
        grid_spec=pltpu.PrefetchScalarGridSpec(
            num_scalar_prefetch=1,
            grid=(LIVE,),
            in_specs=[
                pl.BlockSpec(
                    (1, L, BLOCK), lambda e, place_ref: (place_ref[e] // POOL, place_ref[e] % POOL, 0)
                )
            ],
            out_specs=pl.BlockSpec((BLOCK, L), lambda e, place_ref: (0, e)),
        ),
        out_shape=jax.ShapeDtypeStruct((BLOCK, LIVE * L), jnp.bfloat16),
        compiler_params=pltpu.CompilerParams(vmem_limit_bytes=VMEM),
        cost_estimate=pl.CostEstimate(flops=0, bytes_accessed=4 * LIVE * L * BLOCK, transcendentals=0),
        name="turn",
    )(place, blocks)


def product_kernel(core_ref, factor_ref, *refs):
    bands, quarters = refs[:QUARTERS], refs[QUARTERS : 2 * QUARTERS]
    out_refs, (weighted, total) = refs[2 * QUARTERS : -2], refs[-2:]
    for q, ref in enumerate(quarters):
        for k in range(LIVE // QUARTERS):
            e = q * (LIVE // QUARTERS) + k
            rows = ref[k * L : (k + 1) * L, :].astype(jnp.float32)
            weighted[e * L : (e + 1) * L, :] = (factor_ref[e] * rows).astype(jnp.bfloat16)
    height = BLOCK // QUARTERS
    for q, ref in enumerate(bands):
        total[q * height : (q + 1) * height, :] = jnp.dot(
            ref[...], weighted[...], preferred_element_type=jnp.float32
        )
    core = core_ref[0]
    start = 0
    for c, width in enumerate(WIDTHS):
        end = start + width // TILE

        @pl.when((pl.program_id(0) >= start) & (pl.program_id(0) < end))
        def _(keep_ref=out_refs[2 * c], send_ref=out_refs[2 * c + 1]):
            for z in range(NZ):
                base = z * CORES * ROWS
                mine = pl.multiple_of(base + core * ROWS, 8)
                others = pl.multiple_of(base + (1 - core) * ROWS, 8)
                keep_ref[z] = total[pl.ds(mine, ROWS), :]
                send_ref[z] = total[pl.ds(others, ROWS), :]

        start = end


def product(core, factors, turned, cotangents):
    scalars = pl.BlockSpec(memory_space=pltpu.SMEM)
    out_specs, out_shape = [], []
    start = 0
    for width in WIDTHS:
        tiles = width // TILE

        def at(i, start=start, tiles=tiles):
            return (0, 0, jnp.clip(i - start, 0, tiles - 1))

        out_specs += [pl.BlockSpec((NZ, ROWS, TILE), at)] * 2
        out_shape += [jax.ShapeDtypeStruct((NZ, ROWS, width), jnp.float32)] * 2
        start += tiles
    return pl.pallas_call(
        product_kernel,
        grid=(D // TILE,),
        in_specs=[scalars, scalars]
        + [
            pl.BlockSpec((BLOCK // QUARTERS, LIVE * L), lambda i, q=q: (q, 0)) for q in range(QUARTERS)
        ]
        + [
            pl.BlockSpec((LIVE * L // QUARTERS, TILE), lambda i, q=q: (q, i)) for q in range(QUARTERS)
        ],
        out_specs=out_specs,
        out_shape=out_shape,
        scratch_shapes=[
            pltpu.VMEM((LIVE * L, TILE), jnp.bfloat16),
            pltpu.VMEM((BLOCK, TILE), jnp.float32),
        ],
        compiler_params=pltpu.CompilerParams(vmem_limit_bytes=VMEM),
        cost_estimate=pl.CostEstimate(
            flops=2 * LIVE * L * BLOCK * D, bytes_accessed=24 * 2**20, transcendentals=0
        ),
        name="product",
    )(core, factors, *[turned] * QUARTERS, *[cotangents] * QUARTERS)


def around_z(step):
    return [(i, (i + step * CORES) % N_FSDP) for i in range(N_FSDP)]


def other_core(send):
    return lax.ppermute(send, "fsdp", [(i, i ^ 1) for i in range(N_FSDP)])


def reduce_begin(keep, got):
    z = lax.axis_index("fsdp") // CORES

    def own(offset):
        at = (z + offset) % NZ
        return lax.dynamic_index_in_dim(keep, at, 0, False) + lax.dynamic_index_in_dim(got, at, 0, False)

    half = keep.shape[2] // 2
    far = own(NZ // 2)
    up = lax.ppermute(far[:, :half], "fsdp", around_z(1))
    down = lax.ppermute(far[:, half:], "fsdp", around_z(-1))
    up = jnp.concatenate([up, jnp.zeros_like(up)], 1) + own(NZ // 2 - 1)
    down = jnp.concatenate([jnp.zeros_like(down), down], 1) + own(1 - NZ // 2)
    return own, up, down


def reduce_step(own, up, down, offset):
    up = lax.ppermute(up, "fsdp", around_z(1))
    down = lax.ppermute(down, "fsdp", around_z(-1))
    if offset:
        return up + own(offset), down + own(-offset)
    return up + down + own(0)


def across_dp(value):
    return lax.all_to_all(value, "dp", split_axis=0, concat_axis=0, tiled=True)


def body(hidden, cotangent, counts, noise):
    me = lax.axis_index("dp")
    hidden, cotangent = hidden[0, 0], cotangent[0, 0]
    last = lax.dynamic_index_in_dim(cotangent, jnp.clip(counts[0, 0] - 1, 0, POOL - 1), 0, False)
    told = jnp.broadcast_to(counts[:, :, None], (N_DP, 8, L))
    last, hidden, told = lax.optimization_barrier((last, hidden, told))
    passed = lax.ppermute(last, "dp", [(i, (i + 1) % N_DP) for i in range(N_DP)])
    held = across_dp(told)[:, 0, 0]
    blocks, factors = prepare(hidden, cotangent, counts)

    index = jnp.arange(N_DP, dtype=jnp.int32)
    before = jnp.sum(jnp.where(index[None, :] < index[:, None], held[None, :], 0), axis=1)
    left = jnp.sum(jnp.where(index[None, :] == index[:, None] - 1, held[None, :], 0), axis=1)
    shifted = before > index * BAL
    place = jnp.where(
        shifted,
        jnp.maximum(index - 1, 0) * POOL + jnp.clip(left - 1, 0, POOL - 1),
        index * POOL,
    )
    mine_shifted = jnp.sum(jnp.where(index == me, shifted.astype(jnp.int32), 0)) > 0
    chosen = jnp.where(mine_shifted, passed, cotangent[0])

    chosen, blocks, place, factors = lax.optimization_barrier((chosen, blocks, place, factors))
    cotangents = lax.all_gather(chosen, "dp", axis=0, tiled=True)
    blocks = across_dp(blocks.reshape(N_DP, TOK, BLOCK))
    blocks, factors, place = lax.optimization_barrier((blocks, factors, place))
    factors = across_dp(factors)[:, 0, :POOL].reshape(-1)
    factors = jnp.sum(
        jnp.where(place[:, None] == jnp.arange(N_DP * POOL)[None, :], factors[None, :], 0.0), axis=1
    )
    turned = turn(place, blocks)
    core = (lax.axis_index("fsdp") % CORES).astype(jnp.int32).reshape(1)
    core, factors, turned, cotangents = lax.optimization_barrier((core, factors, turned, cotangents))
    chunks = product(core, factors, turned, cotangents)
    parts, got = [], core
    for keep, send in zip(chunks[::2], chunks[1::2]):
        got, send = lax.optimization_barrier((got, send))
        got = other_core(send)
        parts.append(reduce_begin(keep, got))
    for offset in (2, 1, 0):
        sums = []
        for own, up, down in parts:
            sums.append(reduce_step(own, up, down, offset))
        parts = [(own, *moved) for (own, _, _), moved in zip(parts, sums)] if offset else sums
    return (jnp.concatenate(parts, 1) + noise) / (N_DP * N_FSDP * BAL)


def solution(mesh):
    in_specs = (
        P("dp", "fsdp", None, None, None),
        P("dp", "fsdp", None, None, None),
        P("dp", "fsdp"),
        P(("dp", "fsdp"), None),
    )
    out_specs = P(("dp", "fsdp"), None)
    return jax.shard_map(body, mesh=mesh, in_specs=in_specs, out_specs=out_specs, check_vma=False)
```

```python
import math

import jax
import jax.numpy as jnp
from jax import lax
from jax.experimental import pallas as pl
from jax.experimental.pallas import tpu as pltpu
from jax.sharding import PartitionSpec as P

D = 1792
F = 14336
L = 128
BAL = 1
POOL = 2
N_DP = 16
N_FSDP = 16
CORES = 2
NZ = N_FSDP // CORES
TOK = POOL * L
BLOCK = F // N_DP
ROWS = BLOCK // N_FSDP
LIVE = N_DP * BAL
TILE = 256
QUARTERS = 4
WIDTHS = (768, 1024)
CLIP = math.sqrt(L * F * D)
VMEM = 48 * 2**20


def prepare_kernel(count_ref, hidden_ref, cotangent_ref, blocks_ref, factor_ref, rows_buf, other_buf, gram, sems):
    def load(d):
        return pltpu.make_async_copy(
            hidden_ref.at[:, :, pl.ds(pl.multiple_of(d * BLOCK, L), BLOCK)], rows_buf.at[d], sems.at[0, d]
        )

    def store(d):
        return pltpu.make_async_copy(rows_buf.at[d], blocks_ref.at[d], sems.at[1, d])

    second = pltpu.make_async_copy(cotangent_ref, other_buf, sems.at[2, 0])
    for d in range(N_DP):
        load(d).start()
    second.start()
    gram[...] = jnp.zeros_like(gram)

    def step(d, carry):
        load(d).wait()
        store(d).start()
        rows = rows_buf[d].reshape(TOK, BLOCK)
        gram[...] += lax.dot_general(
            rows, rows, (((1,), (1,)), ((), ())), preferred_element_type=jnp.float32
        )
        return carry

    lax.fori_loop(0, N_DP, step, 0)
    second.wait()
    held = count_ref[0, 0]
    rows = other_buf[...].reshape(TOK, D)
    other = lax.dot_general(rows, rows, (((1,), (1,)), ((), ())), preferred_element_type=jnp.float32)
    both = gram[...] * other
    lane = lax.broadcasted_iota(jnp.int32, (8, L), 1)
    factors = jnp.zeros((8, L), jnp.float32)
    for s in range(POOL):
        span = slice(s * L, (s + 1) * L)
        squared = jnp.sum(both[span, span], axis=(0, 1), keepdims=True)
        norm = jnp.sqrt(jnp.maximum(squared, 0.0))
        factor = CLIP / jnp.maximum(norm, CLIP)
        factor = jnp.where(s < held, factor, jnp.zeros_like(factor))
        factors = jnp.where(lane == s, factor, factors)
    for d in range(N_DP):
        factor_ref[d] = factors
    for d in range(N_DP):
        store(d).wait()


def prepare(hidden, cotangent, held):
    anywhere = pl.BlockSpec(memory_space=pl.ANY)
    whole = pl.BlockSpec(memory_space=pltpu.VMEM)
    return pl.pallas_call(
        prepare_kernel,
        in_specs=[pl.BlockSpec(memory_space=pltpu.SMEM), anywhere, anywhere],
        out_specs=[anywhere, whole],
        out_shape=[
            jax.ShapeDtypeStruct((N_DP, POOL, L, BLOCK), jnp.bfloat16),
            jax.ShapeDtypeStruct((N_DP, 8, L), jnp.float32),
        ],
        scratch_shapes=[
            pltpu.VMEM((N_DP, POOL, L, BLOCK), jnp.bfloat16),
            pltpu.VMEM((POOL, L, D), jnp.bfloat16),
            pltpu.VMEM((TOK, TOK), jnp.float32),
            pltpu.SemaphoreType.DMA((3, N_DP)),
        ],
        compiler_params=pltpu.CompilerParams(vmem_limit_bytes=VMEM + 12 * 2**20),
        cost_estimate=pl.CostEstimate(
            flops=2 * TOK * L * F, bytes_accessed=4 * TOK * F, transcendentals=0
        ),
        name="prepare",
    )(held, hidden, cotangent)


def turn_kernel(place_ref, blocks_ref, out_ref):
    out_ref[...] = blocks_ref[0].T


def turn(place, blocks):
    return pl.pallas_call(
        turn_kernel,
        grid_spec=pltpu.PrefetchScalarGridSpec(
            num_scalar_prefetch=1,
            grid=(LIVE,),
            in_specs=[
                pl.BlockSpec(
                    (1, L, BLOCK), lambda e, place_ref: (place_ref[e] // POOL, place_ref[e] % POOL, 0)
                )
            ],
            out_specs=pl.BlockSpec((BLOCK, L), lambda e, place_ref: (0, e)),
        ),
        out_shape=jax.ShapeDtypeStruct((BLOCK, LIVE * L), jnp.bfloat16),
        compiler_params=pltpu.CompilerParams(vmem_limit_bytes=VMEM),
        cost_estimate=pl.CostEstimate(flops=0, bytes_accessed=4 * LIVE * L * BLOCK, transcendentals=0),
        name="turn",
    )(place, blocks)


def product_kernel(core_ref, factor_ref, turned_ref, *refs):
    quarters, (keep_ref, send_ref, weighted, total) = refs[:QUARTERS], refs[QUARTERS:]
    for q, ref in enumerate(quarters):
        for k in range(LIVE // QUARTERS):
            e = q * (LIVE // QUARTERS) + k
            rows = ref[k * L : (k + 1) * L, :].astype(jnp.float32)
            weighted[e * L : (e + 1) * L, :] = (factor_ref[e] * rows).astype(jnp.bfloat16)
    total[...] = jnp.dot(turned_ref[...], weighted[...], preferred_element_type=jnp.float32)
    core = core_ref[0]
    for z in range(NZ):
        base = z * CORES * ROWS
        mine = pl.multiple_of(base + core * ROWS, 8)
        others = pl.multiple_of(base + (1 - core) * ROWS, 8)
        keep_ref[z] = total[pl.ds(mine, ROWS), :]
        send_ref[z] = total[pl.ds(others, ROWS), :]


def product(core, factors, turned, cotangents, start, width):
    out = jax.ShapeDtypeStruct((NZ, ROWS, width), jnp.float32)
    scalars = pl.BlockSpec(memory_space=pltpu.SMEM)
    return pl.pallas_call(
        product_kernel,
        grid=(width // TILE,),
        in_specs=[scalars, scalars, pl.BlockSpec((BLOCK, LIVE * L), lambda i: (0, 0))]
        + [
            pl.BlockSpec((LIVE * L // QUARTERS, TILE), lambda i, q=q: (q, start // TILE + i))
            for q in range(QUARTERS)
        ],
        out_specs=[pl.BlockSpec((NZ, ROWS, TILE), lambda i: (0, 0, i))] * 2,
        out_shape=[out, out],
        scratch_shapes=[
            pltpu.VMEM((LIVE * L, TILE), jnp.bfloat16),
            pltpu.VMEM((BLOCK, TILE), jnp.float32),
        ],
        compiler_params=pltpu.CompilerParams(vmem_limit_bytes=58 * 2**20),
        cost_estimate=pl.CostEstimate(
            flops=2 * LIVE * L * BLOCK * width, bytes_accessed=12 * 2**20, transcendentals=0
        ),
        name="product",
    )(core, factors, turned, *[cotangents] * QUARTERS)


def around_z(step):
    return [(i, (i + step * CORES) % N_FSDP) for i in range(N_FSDP)]


def other_core(send):
    return lax.ppermute(send, "fsdp", [(i, i ^ 1) for i in range(N_FSDP)])


def reduce_begin(keep, got):
    z = lax.axis_index("fsdp") // CORES

    def own(offset):
        at = (z + offset) % NZ
        return lax.dynamic_index_in_dim(keep, at, 0, False) + lax.dynamic_index_in_dim(got, at, 0, False)

    half = keep.shape[2] // 2
    far = own(NZ // 2)
    up = lax.ppermute(far[:, :half], "fsdp", around_z(1))
    down = lax.ppermute(far[:, half:], "fsdp", around_z(-1))
    up = jnp.concatenate([up, jnp.zeros_like(up)], 1) + own(NZ // 2 - 1)
    down = jnp.concatenate([jnp.zeros_like(down), down], 1) + own(1 - NZ // 2)
    return own, up, down


def reduce_step(own, up, down, offset):
    up = lax.ppermute(up, "fsdp", around_z(1))
    down = lax.ppermute(down, "fsdp", around_z(-1))
    if offset:
        return up + own(offset), down + own(-offset)
    return up + down + own(0)


def across_dp(value):
    return lax.all_to_all(value, "dp", split_axis=0, concat_axis=0, tiled=True)


def body(hidden, cotangent, counts, noise):
    me = lax.axis_index("dp")
    hidden, cotangent = hidden[0, 0], cotangent[0, 0]
    last = lax.dynamic_index_in_dim(cotangent, jnp.clip(counts[0, 0] - 1, 0, POOL - 1), 0, False)
    last, hidden, counts = lax.optimization_barrier((last, hidden, counts))
    passed = lax.ppermute(last, "dp", [(i, (i + 1) % N_DP) for i in range(N_DP)])
    held = across_dp(jnp.broadcast_to(counts[:, :, None], (N_DP, 8, L)))[:, 0, 0]
    blocks, factors = prepare(hidden, cotangent, counts)

    index = jnp.arange(N_DP, dtype=jnp.int32)
    before = jnp.sum(jnp.where(index[None, :] < index[:, None], held[None, :], 0), axis=1)
    left = jnp.sum(jnp.where(index[None, :] == index[:, None] - 1, held[None, :], 0), axis=1)
    shifted = before > index * BAL
    place = jnp.where(
        shifted,
        jnp.maximum(index - 1, 0) * POOL + jnp.clip(left - 1, 0, POOL - 1),
        index * POOL,
    )
    mine_shifted = jnp.sum(jnp.where(index == me, shifted.astype(jnp.int32), 0)) > 0
    chosen = jnp.where(mine_shifted, passed, cotangent[0])

    chosen, blocks, place, factors = lax.optimization_barrier((chosen, blocks, place, factors))
    cotangents = lax.all_gather(chosen, "dp", axis=0, tiled=True)
    blocks = across_dp(blocks.reshape(N_DP, TOK, BLOCK))
    blocks, factors, place = lax.optimization_barrier((blocks, factors, place))
    factors = across_dp(factors)[:, 0, :POOL].reshape(-1)
    factors = jnp.sum(
        jnp.where(place[:, None] == jnp.arange(N_DP * POOL)[None, :], factors[None, :], 0.0), axis=1
    )
    turned = turn(place, blocks)
    core = (lax.axis_index("fsdp") % CORES).astype(jnp.int32).reshape(1)
    core, factors, turned, cotangents = lax.optimization_barrier((core, factors, turned, cotangents))
    parts, got = [], core
    for i, width in enumerate(WIDTHS):
        keep, send = product(core, factors, turned, cotangents, sum(WIDTHS[:i]), width)
        got, send = lax.optimization_barrier((got, send))
        got = other_core(send)
        parts.append(reduce_begin(keep, got))
    for offset in (2, 1, 0):
        sums = []
        for own, up, down in parts:
            sums.append(reduce_step(own, up, down, offset))
        parts = [(own, *moved) for (own, _, _), moved in zip(parts, sums)] if offset else sums
    return (jnp.concatenate(parts, 1) + noise) / (N_DP * N_FSDP * BAL)


def solution(mesh):
    in_specs = (
        P("dp", "fsdp", None, None, None),
        P("dp", "fsdp", None, None, None),
        P("dp", "fsdp"),
        P(("dp", "fsdp"), None),
    )
    out_specs = P(("dp", "fsdp"), None)
    return jax.shard_map(body, mesh=mesh, in_specs=in_specs, out_specs=out_specs, check_vma=False)
```
